256 devices in a mesh: dp: 32 (over y, z_hi, core), tensor: 8 (over x, z_lo).
Axes of the slice: x: 4, y: 4, z: 8 (z_hi: 4, z_lo: 2; z = z_hi * 2 + z_lo), core: 2. Of those that a mesh axis runs over, the one named last changes fastest.
Arguments:
- layer_inputs: bfloat16 [32, 384, 16384], P(None, 'tensor', 'dp'), may hold values from -6 to 6
- out_grads: bfloat16 [16384, 28672], P('dp', 'tensor'), may hold values from -4 to 4
- projector: float32 [12288, 256], P(('dp', 'tensor')), may hold values from -2 to 2
- weights: bfloat16 [12288, 28672], P('dp', 'tensor'), may hold values from -6 to 6
- moment_first: float32 [256, 28672], P('dp', 'tensor'), may hold values from -6 to 6
- moment_second: float32 [256, 28672], P('dp', 'tensor'), may hold values from 0.01 to 1
Outputs:
- new_weights: bfloat16 [12288, 28672], P('dp', 'tensor')
- new_first: float32 [256, 28672], P('dp', 'tensor')
- new_second: float32 [256, 28672], P('dp', 'tensor')
- increment: float32 [12288, 256], P(('dp', 'tensor'))
The draws below stay inside these ranges and needn't reach their ends.
All inputs are finite; a program needn't handle non-finite values.
Results may differ from the reference program's by a relative error of at most 0.019.
Values may be sent and summed in bfloat16 or wider, within the bound.
No kernel may reach another device: no remote copies, remote signals or barrier semaphores. Data moves between devices by JAX's collectives and lax.ppermute only.
A program may use at most 64 MiB of HBM per device.

```python
import math
import jax
import jax.numpy as jnp
from jax import lax

D = 12288
FF = 28672
R = 256
TOKENS = 16384
NBLK = 32
FBLK = 384


def draw_out_grads(key, part):
    key = jax.random.fold_in(key, 17)
    key_base, key_col, key_row = jax.random.split(key, 3)
    row_scale = jnp.exp(jax.random.uniform(key_row, (TOKENS, 1), jnp.float32, math.log(0.5), math.log(2.0)))
    entries = jax.random.truncated_normal(key_base, -4.0, 4.0, (TOKENS, FF), jnp.float32)
    column = jnp.exp(jax.random.uniform(key_col, (1, FF), jnp.float32, math.log(0.3), math.log(3.0)))
    return (entries * column * row_scale * TOKENS ** (-0.5)).astype(jnp.bfloat16)


def draw_projector(key, part):
    key = jax.random.fold_in(key, 29)
    key_base, key_col, key_row = jax.random.split(key, 3)
    entries = jax.random.truncated_normal(key_base, -4.0, 4.0, (D, R), jnp.float32)
    column = jnp.exp(jax.random.uniform(key_col, (1, R), jnp.float32, math.log(0.5), math.log(2.0)))
    position = jnp.arange(D, dtype=jnp.float32).reshape(D, 1) / D
    row_scale = jnp.exp(jax.random.uniform(key_row, (D, 1), jnp.float32, math.log(0.7), math.log(1.4)))
    row_scale = row_scale * (0.6 + 1.2 * position)
    return entries * column * row_scale * D ** (-0.5)


def level_of(key, extent, cuts, smallest, high):
    def one(axis_at, parts):
        steps = jax.random.uniform(jax.random.fold_in(jax.random.fold_in(key, 6), axis_at), (parts,), jnp.float32, smallest / len(cuts), high / len(cuts))
        return jnp.repeat(jnp.exp(steps), extent[axis_at] // parts).reshape((-1,) + (1,) * (len(extent) - axis_at - 1))

    loudness = one(*cuts[0])
    for cut in cuts[1:]:
        loudness = loudness * one(*cut)
    return loudness


def normal_values(key, extent, scale, limit, cuts=(), kind=jnp.bfloat16):
    array = jax.random.normal(key, extent, jnp.float32) * scale
    if len(cuts) > 0:
        array = level_of(key, extent, cuts, -0.22, 0.18) * array
    return jnp.clip(array, min=-limit, max=limit).astype(kind)


def setup_inputs(seed: int = 0) -> dict:
    arg_keys = jax.random.split(jax.random.key(seed), 7)
    return {
        "layer_inputs": normal_values(arg_keys[0], (NBLK, FBLK, TOKENS), 1.0, 6.0, ((1, 8), (2, 32))),
        "out_grads": draw_out_grads(jax.random.fold_in(arg_keys[6], 71), 0),
        "projector": draw_projector(jax.random.fold_in(arg_keys[6], 71), 0),
        "weights": normal_values(arg_keys[3], (D, FF), 1.0, 6.0, ((0, 32), (1, 8))),
        "moment_first": normal_values(arg_keys[4], (R, FF), 1.0, 6.0, ((0, 32), (1, 8)), jnp.float32),
        "moment_second": jnp.clip(jnp.exp(math.log(1.0) - 4.6051702 * jax.random.uniform(arg_keys[5], (R, FF), jnp.float32) ** level_of(arg_keys[5], (R, FF), ((0, 32), (1, 8)), -0.2, 0.2)), 0.01, 1.0),
    }


beta_first = 0.9
beta_second = 0.999
bias_first = 1.0 / (1.0 - 0.9 ** 10)
bias_second = 1.0 / (1.0 - 0.999 ** 10)
epsilon = 1e-08
weight_rate = 2.0
proj_rate = 0.0002

def adam_rows(gradient, first, second):
    new_first = beta_first * first + (1.0 - beta_first) * gradient
    new_second = beta_second * second + (1.0 - beta_second) * gradient * gradient
    update = new_first * bias_first / (jnp.sqrt(new_second * bias_second) + epsilon)
    return (new_first, new_second, update.astype(jnp.bfloat16))

def increment_rows(feature_sum, proj_rows, gram_q, gram_k):
    highest = lax.Precision.HIGHEST
    first_term = jnp.dot(feature_sum, gram_q, precision=highest)
    second_term = jnp.dot(proj_rows, gram_k, precision=highest)
    return proj_rate * (4.0 * feature_sum - 2.0 * first_term - 2.0 * second_term)

def reference(layer_inputs, out_grads, projector, weights, moment_first, moment_second):
    features = layer_inputs.reshape(D, TOKENS)
    proj_half = projector.astype(jnp.bfloat16)
    latent = jnp.dot(features.T, proj_half, preferred_element_type=jnp.float32).astype(jnp.bfloat16)
    gradient = jnp.dot(latent.T, out_grads, preferred_element_type=jnp.float32)
    grad_half = gradient.astype(jnp.bfloat16)
    new_first, new_second, update = adam_rows(gradient, moment_first, moment_second)
    change = jnp.dot(proj_half, update, preferred_element_type=jnp.float32)
    new_weights = (weights.astype(jnp.float32) - weight_rate * change).astype(jnp.bfloat16)
    token_rank = jnp.dot(out_grads, grad_half.T, preferred_element_type=jnp.float32).astype(jnp.bfloat16)
    gram_k = jnp.dot(grad_half, grad_half.T, preferred_element_type=jnp.float32)
    gram_q = jnp.dot(proj_half.T, proj_half, preferred_element_type=jnp.float32)
    feature_sum = jnp.dot(features, token_rank, preferred_element_type=jnp.float32)
    increment = increment_rows(feature_sum, projector, gram_q, gram_k)
    return (new_weights, new_first, new_second, increment)
```

```python
import jax
import jax.numpy as jnp
from jax import lax
from jax.experimental import pallas as pl
from jax.experimental.pallas import tpu as pltpu
from jax.sharding import PartitionSpec as P

beta_first = 0.9
beta_second = 0.999
bias_first = 1.0 / (1.0 - 0.9**10)
bias_second = 1.0 / (1.0 - 0.999**10)
epsilon = 1e-08
weight_rate = 2.0
proj_rate = 0.0002

bf16 = jnp.bfloat16
f32 = jnp.float32
HIGHEST = lax.Precision.HIGHEST
NY, NZ, NC = 4, 4, 2
NX, NL = 4, 2
TN = (((0,), (0,)), ((), ()))
NT = (((1,), (1,)), ((), ()))
VMEM_LIMIT = 40 * 1024 * 1024


def dp_pairs(dy, dz, dc):
    return [
        (
            (y * NZ + z) * NC + c,
            (((y + dy) % NY) * NZ + (z + dz) % NZ) * NC + (c + dc) % NC,
        )
        for y in range(NY)
        for z in range(NZ)
        for c in range(NC)
    ]


def tensor_pairs(dx, dl):
    return [
        (x * NL + l, ((x + dx) % NX) * NL + (l + dl) % NL)
        for x in range(NX)
        for l in range(NL)
    ]


def send_y(block, k):
    return lax.ppermute(block, "dp", dp_pairs(k, 0, 0))


def send_z(block, k):
    return lax.ppermute(block, "dp", dp_pairs(0, k, 0))


def send_core(block):
    return lax.ppermute(block, "dp", dp_pairs(0, 0, 1))


def send_x(block, k):
    return lax.ppermute(block, "tensor", tensor_pairs(k, 0))


def send_l(block):
    return lax.ppermute(block, "tensor", tensor_pairs(0, 1))


def gather_ring(block, send, axis=0):
    got = {k: send(block, k) for k in (1, 3, 2)}
    return jnp.concatenate([block, got[3], got[2], got[1]], axis=axis)


def gather_dp(block):
    quarter = gather_ring(block, send_z)
    half = gather_ring(quarter, send_y)
    return jnp.concatenate([half, send_core(half)], axis=0)


def gather_tensor(block):
    pair = jnp.concatenate([block, send_l(block)], axis=0)
    return gather_ring(pair, send_x)


def reduce_ring(rows, send, kind):
    n = rows.shape[0] // 4
    got = [send(rows[k * n : (k + 1) * n].astype(kind), k) for k in (1, 3, 2)]
    total = rows[:n].astype(f32)
    for block in got:
        total = total + block.astype(f32)
    return total


def one_hot(left, right):
    return (left[:, None] == right[None, :]).astype(bf16)


def latent_kernel(pos, proj_ref, x_ref, keep_ref, s1_ref, s2_ref, s3_ref, gram_ref, total, gram):
    step = pl.program_id(0)
    z = pos[1]
    x = jnp.concatenate([x_ref[0, lax.rem(z + k, NZ), 0] for k in range(NZ)], axis=0)
    p = proj_ref[...]
    part = lax.dot_general(p, x, TN, preferred_element_type=f32)
    gram_part = lax.dot_general(p, p, TN, preferred_element_type=f32)

    @pl.when(step == 0)
    def _():
        total[...] = part
        gram[...] = gram_part

    @pl.when(step > 0)
    def _():
        total[...] += part
        gram[...] += gram_part

    @pl.when(step == pl.num_programs(0) - 1)
    def _():
        keep_ref[...] = total[0:64, :]
        s1_ref[...] = total[64:128, :].astype(bf16)
        s2_ref[...] = total[128:192, :].astype(bf16)
        s3_ref[...] = total[192:256, :].astype(bf16)
        gram_ref[...] = gram[...]


def latent_parts(pos, proj_rel, x_view):
    tokens = x_view.shape[-1]
    rows = NZ * x_view.shape[3]
    ranks = proj_rel.shape[1]
    quarter = ranks // 4
    whole = lambda *shape: pl.BlockSpec(shape, lambda g, pos: (0,) * len(shape))
    return pl.pallas_call(
        latent_kernel,
        grid_spec=pltpu.PrefetchScalarGridSpec(
            num_scalar_prefetch=1,
            grid=(NC * NY,),
            in_specs=[
                pl.BlockSpec((rows, ranks), lambda g, pos: (g, 0)),
                pl.BlockSpec(
                    (1, NZ, 1, x_view.shape[3], tokens),
                    lambda g, pos: (
                        lax.rem(pos[0] + lax.rem(g, NY), NY),
                        0,
                        lax.rem(pos[2] + lax.div(g, NY), NC),
                        0,
                        0,
                    ),
                ),
            ],
            out_specs=[
                whole(quarter, tokens),
                whole(quarter, tokens),
                whole(quarter, tokens),
                whole(quarter, tokens),
                whole(ranks, ranks),
            ],
            scratch_shapes=[pltpu.VMEM((ranks, tokens), f32), pltpu.VMEM((ranks, ranks), f32)],
        ),
        out_shape=[
            jax.ShapeDtypeStruct((quarter, tokens), f32),
            jax.ShapeDtypeStruct((quarter, tokens), bf16),
            jax.ShapeDtypeStruct((quarter, tokens), bf16),
            jax.ShapeDtypeStruct((quarter, tokens), bf16),
            jax.ShapeDtypeStruct((ranks, ranks), f32),
        ],
        compiler_params=pltpu.CompilerParams(vmem_limit_bytes=VMEM_LIMIT),
        name="latent",
    )(pos, proj_rel, x_view)


def feature_kernel(pos, x_ref, proj_ref, token_ref, gram_ref, out_ref):
    z = pos[1]
    x = jnp.concatenate([x_ref[0, lax.rem(z + k, NZ), 0] for k in range(NZ)], axis=0)
    value = jnp.dot(x, token_ref[...], preferred_element_type=f32)
    value = value + jnp.dot(proj_ref[...], gram_ref[...], preferred_element_type=f32)
    out_ref[...] = value.astype(out_ref.dtype)


def feature_half(pos, x_view, proj_rel, token, gram_rows, core_step, kind):
    tokens = x_view.shape[-1]
    rows = NZ * x_view.shape[3]
    ranks = proj_rel.shape[1]
    return pl.pallas_call(
        feature_kernel,
        grid_spec=pltpu.PrefetchScalarGridSpec(
            num_scalar_prefetch=1,
            grid=(NY,),
            in_specs=[
                pl.BlockSpec(
                    (1, NZ, 1, x_view.shape[3], tokens),
                    lambda g, pos: (
                        lax.rem(pos[0] + g, NY),
                        0,
                        lax.rem(pos[2] + core_step, NC),
                        0,
                        0,
                    ),
                ),
                pl.BlockSpec((rows, ranks), lambda g, pos: (g + core_step * NY, 0)),
                pl.BlockSpec((tokens, ranks), lambda g, pos: (0, 0)),
                pl.BlockSpec((ranks, ranks), lambda g, pos: (0, 0)),
            ],
            out_specs=pl.BlockSpec((rows, ranks), lambda g, pos: (g, 0)),
        ),
        out_shape=jax.ShapeDtypeStruct((NY * rows, ranks), kind),
        compiler_params=pltpu.CompilerParams(vmem_limit_bytes=VMEM_LIMIT),
        name="feature",
    )(pos, x_view, proj_rel, token, gram_rows)


def weights_kernel(proj_ref, update_ref, weights_ref, out_ref):
    change = jnp.dot(proj_ref[...], update_ref[...], preferred_element_type=f32)
    out_ref[...] = (weights_ref[...].astype(f32) - weight_rate * change).astype(bf16)


def weights_step(proj_block, update, weights):
    rows, cols = weights.shape
    ranks = proj_block.shape[1]
    width = cols // 7
    return pl.pallas_call(
        weights_kernel,
        grid=(7,),
        in_specs=[
            pl.BlockSpec((rows, ranks), lambda g: (0, 0)),
            pl.BlockSpec((ranks, width), lambda g: (0, g)),
            pl.BlockSpec((rows, width), lambda g: (0, g)),
        ],
        out_specs=pl.BlockSpec((rows, width), lambda g: (0, g)),
        out_shape=jax.ShapeDtypeStruct((rows, cols), bf16),
        compiler_params=pltpu.CompilerParams(vmem_limit_bytes=VMEM_LIMIT),
        name="weights",
    )(proj_block, update, weights)


def adam_rows(gradient, first, second):
    new_first = beta_first * first + (1.0 - beta_first) * gradient
    new_second = beta_second * second + (1.0 - beta_second) * gradient * gradient
    update = new_first * bias_first / (jnp.sqrt(new_second * bias_second) + epsilon)
    return (new_first, new_second, update.astype(bf16))


def body(layer_inputs, out_grads, projector, weights, moment_first, moment_second):
    blocks, block_width, tokens = layer_inputs.shape
    ranks = projector.shape[1]
    dp = lax.axis_index("dp")
    tensor = lax.axis_index("tensor")
    y, z, c = dp // (NZ * NC), (dp // NC) % NZ, dp % NC
    x, l = tensor // NL, tensor % NL
    pos = jnp.stack([y, z, c]).astype(jnp.int32)
    x_view = layer_inputs.reshape(NY, NZ, NC, block_width, tokens)

    rank = jnp.arange(ranks, dtype=jnp.int32)
    rank_q = ((rank // 64 + x) % NX) * 64 + ((rank // 32 + l) % NL) * 32 + rank % 32
    rank_p = (
        ((rank // 32 + y) % NY) * 64
        + ((rank // 8 + z) % NZ) * 16
        + ((rank // 128 + c) % NC) * 8
        + rank % 8
    )
    p_from_q = one_hot(rank_p, rank_q)
    p_from_r = one_hot(rank_p, rank)
    token = jnp.arange(tokens, dtype=jnp.int32)
    token_q = ((token // 128 + x) % NX) * 128 + ((token // 64 + l) % NL) * 64 + token % 64

    proj_half = projector.astype(bf16)
    proj_q = jnp.dot(proj_half, one_hot(rank, rank_q), preferred_element_type=f32).astype(bf16)
    proj_p = lax.dot_general(proj_half, p_from_r, NT, preferred_element_type=f32).astype(bf16)
    proj_rel = gather_dp(proj_q)

    keep, s1, s2, s3, gram_part = latent_parts(pos, proj_rel, x_view)
    total = keep
    for k, part in ((1, s1), (3, s3), (2, s2)):
        total = total + send_x(part, k).astype(f32)
    latent = total[:32] + send_l(total[32:].astype(bf16)).astype(f32)
    latent_q = gather_tensor(latent.astype(bf16))
    latent_p = jnp.dot(p_from_q, latent_q, preferred_element_type=f32).astype(bf16)

    half = ranks // 2
    grad_send = jnp.dot(latent_p[half:], out_grads, preferred_element_type=f32).astype(bf16)
    grad_keep = jnp.dot(latent_p[:half], out_grads, preferred_element_type=f32)
    total = grad_keep + send_core(grad_send).astype(f32)
    total = reduce_ring(total, send_y, bf16)
    gradient = reduce_ring(total, send_z, bf16)
    grad_half = gradient.astype(bf16)
    new_first, new_second, update = adam_rows(gradient, moment_first, moment_second)
    grad_p = gather_dp(grad_half)

    gram_cols = lax.dot_general(
        gram_part, one_hot(rank, rank_q).astype(f32), NT, precision=HIGHEST
    )
    total = reduce_ring(gram_cols, send_x, f32)
    gram_own = total[:32] + send_l(total[32:])
    gram_q = gather_tensor(gram_own)
    mix = 4.0 * p_from_r.astype(f32) - 2.0 * jnp.dot(
        p_from_q.astype(f32), gram_q, precision=HIGHEST
    )

    token_part = lax.dot_general(out_grads, grad_p, NT, preferred_element_type=f32).astype(bf16)
    token_rel = jnp.dot(one_hot(token_q, token), token_part, preferred_element_type=f32)
    gram_rows = lax.dot_general(grad_half, grad_p, NT, preferred_element_type=f32)
    n = tokens // 4
    got = [
        send_x(jnp.concatenate([token_rel[k * n : (k + 1) * n], gram_rows]).astype(bf16), k)
        for k in (1, 3, 2)
    ]
    total = jnp.concatenate([token_rel[:n], gram_rows])
    for block in got:
        total = total + block.astype(f32)
    n = n // 2
    got = send_l(total[n:].astype(bf16)).astype(f32)
    token_own = total[:n] + got[:n]
    gram_own = total[2 * n :] + got[n:]
    token_mixed = jnp.dot(token_own, mix, precision=HIGHEST).astype(bf16)
    token_all = gather_tensor(token_mixed)
    token_true = jnp.dot(
        one_hot(token, token_q), token_all, preferred_element_type=f32
    ).astype(bf16)
    gram_own = -2.0 * jnp.dot(gram_own, p_from_r.astype(f32), precision=HIGHEST)
    own_rank = dp * 8 + jnp.arange(8, dtype=jnp.int32)
    gram_place = jnp.dot(
        one_hot(rank_q, own_rank), gram_own.astype(bf16), preferred_element_type=f32
    ).astype(bf16)

    feat_send = feature_half(pos, x_view, proj_rel, token_true, gram_place, 1, bf16)
    feat_keep = feature_half(pos, x_view, proj_rel, token_true, gram_place, 0, f32)
    total = feat_keep + send_core(feat_send).astype(f32)
    total = reduce_ring(total, send_y, bf16)
    increment = proj_rate * reduce_ring(total, send_z, bf16)

    place = jnp.arange(8 * projector.shape[0], dtype=jnp.int32)
    place_q = (
        ((place // 96 + x) % NX) * 96 + ((place // 48 + l) % NL) * 48 + place % 48
    )
    proj_block = jnp.dot(
        one_hot(place, place_q), gather_tensor(proj_p), preferred_element_type=f32
    ).astype(bf16)
    update_p = gather_dp(update)
    new_weights = weights_step(proj_block, update_p, weights)
    return (new_weights, new_first, new_second, increment)


def solution(mesh):
    placed = (
        P(None, "tensor", "dp"),
        P("dp", "tensor"),
        P(("dp", "tensor"), None),
        P("dp", "tensor"),
        P("dp", "tensor"),
        P("dp", "tensor"),
    )
    return jax.shard_map(
        body,
        mesh=mesh,
        in_specs=placed,
        out_specs=(
            P("dp", "tensor"),
            P("dp", "tensor"),
            P("dp", "tensor"),
            P(("dp", "tensor"), None),
        ),
        check_vma=False,
    )
```

```python
import jax
import jax.numpy as jnp
from jax import lax
from jax.experimental import pallas as pl
from jax.experimental.pallas import tpu as pltpu
from jax.sharding import PartitionSpec as P

beta_first = 0.9
beta_second = 0.999
bias_first = 1.0 / (1.0 - 0.9**10)
bias_second = 1.0 / (1.0 - 0.999**10)
epsilon = 1e-08
weight_rate = 2.0
proj_rate = 0.0002

bf16 = jnp.bfloat16
f32 = jnp.float32
HIGHEST = lax.Precision.HIGHEST
NY, NZ, NC = 4, 4, 2
NX, NL = 4, 2
TN = (((0,), (0,)), ((), ()))
NT = (((1,), (1,)), ((), ()))
MIB = 1024 * 1024


def dp_pairs(dy, dz, dc):
    return [
        (
            (y * NZ + z) * NC + c,
            (((y + dy) % NY) * NZ + (z + dz) % NZ) * NC + (c + dc) % NC,
        )
        for y in range(NY)
        for z in range(NZ)
        for c in range(NC)
    ]


def send_y(block, k):
    return lax.ppermute(block, "dp", dp_pairs(k, 0, 0))


def send_z(block, k):
    return lax.ppermute(block, "dp", dp_pairs(0, k, 0))


def send_core(block):
    return lax.ppermute(block, "dp", dp_pairs(0, 0, 1))


def send_xor(block, bit):
    return lax.ppermute(block, "tensor", [(j, j ^ bit) for j in range(NX * NL)])


def ring_blocks(block, send):
    got = {k: send(block, k) for k in (1, 3, 2)}
    return jnp.concatenate([block, got[3], got[2], got[1]], axis=0), got[1]


def gather_ring(block, send):
    return ring_blocks(block, send)[0]


def after(value, trigger):
    return lax.optimization_barrier((value, trigger))[0]


def split_high(value):
    high = value.astype(bf16)
    return high, (value - high.astype(f32)).astype(bf16)


def side_step(gram, rows, mask, trigger):
    n = gram.shape[0]
    eye = jnp.eye(n, dtype=f32)
    high, low = split_high(gram)
    rest = jnp.sum(low.astype(f32) * eye, axis=0).astype(bf16)
    payload = jnp.concatenate([high, jnp.broadcast_to(rest, (16, n)), rows], axis=0)
    got = send_xor(after(payload, trigger), mask)
    gram = gram + got[:n].astype(f32) + eye * got[n : n + 1].astype(f32)
    return gram, jnp.concatenate([rows, got[n + 16 :]], axis=0)


def split_sum(part):
    n = NX * NL
    rows, cols = part.shape
    got = lax.all_to_all(part.astype(bf16).reshape(n, rows // n, cols), "tensor", 0, 0)
    return jnp.sum(got.astype(f32), axis=0).astype(bf16)


def spread(own, extra=None):
    n = NX * NL
    rows, cols = own.shape
    blocks = jnp.broadcast_to(own, (n, rows, cols))
    if extra is not None:
        extra_rows = extra.shape[1]
        extra = jnp.pad(extra, ((0, 0), (0, rows - extra_rows), (0, 0)))
        blocks = jnp.concatenate([blocks, extra], axis=1)
    got = lax.all_to_all(blocks, "tensor", 0, 0)
    whole = got[:, :rows].reshape(n * rows, cols)
    return whole if extra is None else (whole, got[:, rows : rows + extra_rows])


def reduce_blocks(rows, send, beside=None):
    n = rows.shape[0] // 4
    got = [send(rows[k * n : (k + 1) * n].astype(bf16), k) for k in (1, 3, 2)]
    total = rows[:n].astype(f32)
    if beside is not None:
        total = after(total, beside)
    for block in got:
        total = total + block.astype(f32)
    return total, got[0]


def reduce_ring(rows, send):
    return reduce_blocks(rows, send)[0]


def one_hot(left, right):
    return (left[:, None] == right[None, :]).astype(bf16)


def turn_kernel(pos, x_ref, out_ref):
    z = pos[1]
    n = x_ref.shape[3]
    for k in range(NZ):
        out_ref[pl.ds(k * n, n), :] = x_ref[0, lax.rem(z + k, NZ), 0]


def turn_blocks(pos, x_view):
    block_width, tokens = x_view.shape[3:]
    rows = NZ * block_width
    return pl.pallas_call(
        turn_kernel,
        grid_spec=pltpu.PrefetchScalarGridSpec(
            num_scalar_prefetch=1,
            grid=(NC * NY,),
            in_specs=[
                pl.BlockSpec(
                    (1, NZ, 1, block_width, tokens),
                    lambda g, pos: (
                        lax.rem(pos[0] + lax.rem(g, NY), NY),
                        0,
                        lax.rem(pos[2] + lax.div(g, NY), NC),
                        0,
                        0,
                    ),
                ),
            ],
            out_specs=pl.BlockSpec((rows, tokens), lambda g, pos: (g, 0)),
        ),
        out_shape=jax.ShapeDtypeStruct((NC * NY * rows, tokens), bf16),
        compiler_params=pltpu.CompilerParams(vmem_limit_bytes=24 * MIB),
        cost_estimate=pl.CostEstimate(flops=0, bytes_accessed=12000000, transcendentals=0),
        name="turn",
    )(pos, x_view)


def gradient_kernel(latent_ref, cot_ref, keep_ref, send_ref):
    half = keep_ref.shape[0]
    for at in range(0, cot_ref.shape[1], 512):
        cols = pl.ds(at, 512)
        part = jnp.dot(latent_ref[...], cot_ref[:, cols], preferred_element_type=f32)
        keep_ref[:, cols] = part[:half]
        send_ref[:, cols] = part[half:].astype(bf16)


def gradient_parts(latent, out_grads):
    ranks, tokens = latent.shape
    cols = out_grads.shape[1]
    half = ranks // 2
    local = pl.BlockSpec(memory_space=pltpu.VMEM)
    return pl.pallas_call(
        gradient_kernel,
        in_specs=[local, local],
        out_specs=[local, local],
        out_shape=[
            jax.ShapeDtypeStruct((half, cols), f32),
            jax.ShapeDtypeStruct((half, cols), bf16),
        ],
        compiler_params=pltpu.CompilerParams(vmem_limit_bytes=24 * MIB),
        cost_estimate=pl.CostEstimate(
            flops=2 * ranks * tokens * cols, bytes_accessed=6500000, transcendentals=0
        ),
        name="gradient",
    )(latent, out_grads)


def weights_kernel(proj_ref, update_ref, weights_ref, out_ref):
    change = jnp.dot(proj_ref[...], update_ref[...], preferred_element_type=f32)
    out_ref[...] = (weights_ref[...].astype(f32) - weight_rate * change).astype(bf16)


def weights_step(proj_block, update, weights):
    rows, cols = weights.shape
    ranks = proj_block.shape[1]
    width = cols // 4
    return pl.pallas_call(
        weights_kernel,
        grid=(4,),
        in_specs=[
            pl.BlockSpec((rows, ranks), lambda g: (0, 0)),
            pl.BlockSpec((ranks, width), lambda g: (0, g)),
            pl.BlockSpec((rows, width), lambda g: (0, g)),
        ],
        out_specs=pl.BlockSpec((rows, width), lambda g: (0, g)),
        out_shape=jax.ShapeDtypeStruct((rows, cols), bf16),
        compiler_params=pltpu.CompilerParams(vmem_limit_bytes=56 * MIB),
        cost_estimate=pl.CostEstimate(
            flops=2 * rows * cols * ranks, bytes_accessed=8000000, transcendentals=0
        ),
        name="weights",
    )(proj_block, update, weights)


def adam_rows(gradient, first, second):
    new_first = beta_first * first + (1.0 - beta_first) * gradient
    new_second = beta_second * second + (1.0 - beta_second) * gradient * gradient
    update = new_first * bias_first / (jnp.sqrt(new_second * bias_second) + epsilon)
    return (new_first, new_second, update.astype(bf16))


def body(layer_inputs, out_grads, projector, weights, moment_first, moment_second):
    blocks, block_width, tokens = layer_inputs.shape
    ranks = projector.shape[1]
    dp = lax.axis_index("dp")
    tensor = lax.axis_index("tensor")
    y, z, c = dp // (NZ * NC), (dp // NC) % NZ, dp % NC
    pos = jnp.stack([y, z, c]).astype(jnp.int32)

    rank = jnp.arange(ranks, dtype=jnp.int32)
    rank_p = (
        ((rank // 32 + y) % NY) * 64
        + ((rank // 8 + z) % NZ) * 16
        + ((rank // 128 + c) % NC) * 8
        + rank % 8
    )
    p_from_r = one_hot(rank_p, rank)

    proj_half = projector.astype(bf16)
    quarter = gather_ring(proj_half, send_z)
    x_rel = turn_blocks(pos, layer_inputs.reshape(NY, NZ, NC, block_width, tokens))
    quarter, x_rel = lax.optimization_barrier((quarter, x_rel))
    proj_rel = gather_ring(quarter, send_y)
    proj_rel = jnp.concatenate([proj_rel, send_core(proj_rel)], axis=0)

    latent_own = split_sum(lax.dot_general(proj_rel, x_rel, TN, preferred_element_type=f32))
    gram_part = lax.dot_general(proj_rel, proj_rel, TN, preferred_element_type=f32)
    latent = spread(latent_own)
    latent_p = jnp.dot(p_from_r, latent, preferred_element_type=f32).astype(bf16)

    grad_keep, grad_send = gradient_parts(latent_p, out_grads)
    total = grad_keep + send_core(grad_send).astype(f32)
    total, first_got = reduce_blocks(total, send_y)
    side = side_step(gram_part, proj_half, 1, first_got)
    total, *side = lax.optimization_barrier((total, *side))
    gradient, first_got = reduce_blocks(total, send_z)
    side = side_step(*side, 2, first_got)
    grad_half = gradient.astype(bf16)
    new_first, new_second, update = adam_rows(gradient, moment_first, moment_second)
    grad_own, first_got = ring_blocks(grad_half, send_z)
    grad_own, *side = lax.optimization_barrier((grad_own, *side))
    update_all = lax.all_gather(update, "dp", axis=0, tiled=True)
    grad_own, first_got = ring_blocks(grad_own, send_y)
    side = side_step(*side, 6, first_got)
    grad_own, gram_q, proj_rows = lax.optimization_barrier((grad_own, *side))
    grad_p = jnp.concatenate([grad_own, send_core(grad_own)], axis=0)
    place = jnp.arange(8 * projector.shape[0], dtype=jnp.int32)
    block = place // block_width
    place_q = (block ^ ((block & 4) >> 1) ^ tensor) * block_width + place % block_width
    proj_block = jnp.dot(
        one_hot(place, place_q), proj_rows, preferred_element_type=f32
    ).astype(bf16)
    proj_block_p = lax.dot_general(
        proj_block, p_from_r, NT, preferred_element_type=f32
    ).astype(bf16)

    token_own = split_sum(lax.dot_general(grad_p, out_grads, NT, preferred_element_type=f32))
    gram_k = lax.dot_general(grad_p, grad_p, NT, preferred_element_type=f32).astype(bf16)
    second_part = jnp.dot(proj_block_p, gram_k, preferred_element_type=f32).astype(bf16)
    token_p, second = spread(token_own, second_part.reshape(NX * NL, -1, tokens))
    mix = 4.0 * jnp.eye(ranks, dtype=f32) - 2.0 * gram_q
    mix_p = jnp.concatenate(
        [
            jnp.dot(p_from_r, part, preferred_element_type=f32).astype(bf16)
            for part in split_high(mix)
        ],
        axis=0,
    )
    token_r = lax.dot_general(
        mix_p, jnp.concatenate([token_p, token_p], axis=0), TN, preferred_element_type=f32
    ).astype(bf16)

    n = x_rel.shape[0] // 2
    feat_send = lax.dot_general(x_rel[n:], token_r, NT, preferred_element_type=f32)
    feat_keep = lax.dot_general(x_rel[:n], token_r, NT, preferred_element_type=f32)
    total = feat_keep + send_core(feat_send.astype(bf16)).astype(f32)
    total = reduce_ring(total, send_y)
    new_weights = weights_step(proj_block, update_all, weights)
    feature_sum = reduce_blocks(total, send_z, new_weights)[0]

    second = jnp.sum(second.astype(f32), axis=0).reshape(block_width, ranks)
    second = jnp.dot(second, p_from_r.astype(f32), precision=HIGHEST)
    increment = proj_rate * (feature_sum - 2.0 * second)
    return (new_weights, new_first, new_second, increment)


def solution(mesh):
    placed = (
        P(None, "tensor", "dp"),
        P("dp", "tensor"),
        P(("dp", "tensor"), None),
        P("dp", "tensor"),
        P("dp", "tensor"),
        P("dp", "tensor"),
    )
    return jax.shard_map(
        body,
        mesh=mesh,
        in_specs=placed,
        out_specs=(
            P("dp", "tensor"),
            P("dp", "tensor"),
            P("dp", "tensor"),
            P(("dp", "tensor"), None),
        ),
        check_vma=False,
    )
```

```python
import jax
import jax.numpy as jnp
from jax import lax
from jax.experimental import pallas as pl
from jax.experimental.pallas import tpu as pltpu
from jax.sharding import PartitionSpec as P

beta_first = 0.9
beta_second = 0.999
bias_first = 1.0 / (1.0 - 0.9**10)
bias_second = 1.0 / (1.0 - 0.999**10)
epsilon = 1e-08
weight_rate = 2.0
proj_rate = 0.0002

bf16 = jnp.bfloat16
f32 = jnp.float32
HIGHEST = lax.Precision.HIGHEST
NY, NZ, NC = 4, 4, 2
NX, NL = 4, 2
TN = (((0,), (0,)), ((), ()))
NT = (((1,), (1,)), ((), ()))
MIB = 1024 * 1024


def dp_pairs(dy, dz, dc):
    return [
        (
            (y * NZ + z) * NC + c,
            (((y + dy) % NY) * NZ + (z + dz) % NZ) * NC + (c + dc) % NC,
        )
        for y in range(NY)
        for z in range(NZ)
        for c in range(NC)
    ]


def send_y(block, k):
    return lax.ppermute(block, "dp", dp_pairs(k, 0, 0))


def send_z(block, k):
    return lax.ppermute(block, "dp", dp_pairs(0, k, 0))


def send_core(block):
    return lax.ppermute(block, "dp", dp_pairs(0, 0, 1))


def send_xor(block, bit):
    return lax.ppermute(block, "tensor", [(j, j ^ bit) for j in range(NX * NL)])


def ring_blocks(block, send):
    got = {k: send(block, k) for k in (2, 1, 3)}
    return jnp.concatenate([block, got[3], got[2], got[1]], axis=0), got[1]


def gather_ring(block, send):
    return ring_blocks(block, send)[0]


def after(value, trigger):
    return lax.optimization_barrier((value, trigger))[0]


def split_high(value):
    high = value.astype(bf16)
    return high, (value - high.astype(f32)).astype(bf16)


def side_step(gram, rows, mask):
    n = gram.shape[0]
    eye = jnp.eye(n, dtype=f32)
    high, low = split_high(gram)
    rest = jnp.sum(low.astype(f32) * eye, axis=0).astype(bf16)
    payload = jnp.concatenate([high, jnp.broadcast_to(rest, (16, n)), rows], axis=0)
    got = send_xor(payload, mask)
    gram = gram + got[:n].astype(f32) + eye * got[n : n + 1].astype(f32)
    return gram, jnp.concatenate([rows, got[n + 16 :]], axis=0)


def split_sum(part):
    n = NX * NL
    rows, cols = part.shape
    got = lax.all_to_all(part.astype(bf16).reshape(n, rows // n, cols), "tensor", 0, 0)
    return jnp.sum(got.astype(f32), axis=0).astype(bf16)


def spread(own, extra=None):
    n = NX * NL
    rows, cols = own.shape
    blocks = jnp.broadcast_to(own, (n, rows, cols))
    if extra is not None:
        extra_rows = extra.shape[1]
        extra = jnp.pad(extra, ((0, 0), (0, rows - extra_rows), (0, 0)))
        blocks = jnp.concatenate([blocks, extra], axis=1)
    got = lax.all_to_all(blocks, "tensor", 0, 0)
    whole = got[:, :rows].reshape(n * rows, cols)
    return whole if extra is None else (whole, got[:, rows : rows + extra_rows])


def reduce_blocks(rows, send, beside=None):
    n = rows.shape[0] // 4
    got = [send(rows[k * n : (k + 1) * n].astype(bf16), k) for k in (2, 1, 3)]
    total = rows[:n].astype(f32)
    if beside is not None:
        total = after(total, beside)
    for block in got:
        total = total + block.astype(f32)
    return total, got[1]


def reduce_ring(rows, send):
    return reduce_blocks(rows, send)[0]


def one_hot(left, right):
    return (left[:, None] == right[None, :]).astype(bf16)


def turn_kernel(pos, x_ref, out_ref):
    z = pos[1]
    n = x_ref.shape[3]
    for k in range(NZ):
        out_ref[pl.ds(k * n, n), :] = x_ref[0, lax.rem(z + k, NZ), 0]


def turn_blocks(pos, x_view):
    block_width, tokens = x_view.shape[3:]
    rows = NZ * block_width
    return pl.pallas_call(
        turn_kernel,
        grid_spec=pltpu.PrefetchScalarGridSpec(
            num_scalar_prefetch=1,
            grid=(NC * NY,),
            in_specs=[
                pl.BlockSpec(
                    (1, NZ, 1, block_width, tokens),
                    lambda g, pos: (
                        lax.rem(pos[0] + lax.rem(g, NY), NY),
                        0,
                        lax.rem(pos[2] + lax.div(g, NY), NC),
                        0,
                        0,
                    ),
                ),
            ],
            out_specs=pl.BlockSpec((rows, tokens), lambda g, pos: (g, 0)),
        ),
        out_shape=jax.ShapeDtypeStruct((NC * NY * rows, tokens), bf16),
        compiler_params=pltpu.CompilerParams(vmem_limit_bytes=24 * MIB),
        cost_estimate=pl.CostEstimate(flops=0, bytes_accessed=12000000, transcendentals=0),
        name="turn",
    )(pos, x_view)


def gradient_kernel(latent_ref, cot_ref, keep_ref, send_ref):
    half = keep_ref.shape[0]
    for at in range(0, cot_ref.shape[1], 512):
        cols = pl.ds(at, 512)
        part = jnp.dot(latent_ref[...], cot_ref[:, cols], preferred_element_type=f32)
        keep_ref[:, cols] = part[:half]
        send_ref[:, cols] = part[half:].astype(bf16)


def gradient_parts(latent, out_grads):
    ranks, tokens = latent.shape
    cols = out_grads.shape[1]
    half = ranks // 2
    local = pl.BlockSpec(memory_space=pltpu.VMEM)
    return pl.pallas_call(
        gradient_kernel,
        in_specs=[local, local],
        out_specs=[local, local],
        out_shape=[
            jax.ShapeDtypeStruct((half, cols), f32),
            jax.ShapeDtypeStruct((half, cols), bf16),
        ],
        compiler_params=pltpu.CompilerParams(vmem_limit_bytes=24 * MIB),
        cost_estimate=pl.CostEstimate(
            flops=2 * ranks * tokens * cols, bytes_accessed=6500000, transcendentals=0
        ),
        name="gradient",
    )(latent, out_grads)


def weights_kernel(proj_ref, update_ref, weights_ref, out_ref):
    change = jnp.dot(proj_ref[...], update_ref[...], preferred_element_type=f32)
    out_ref[...] = (weights_ref[...].astype(f32) - weight_rate * change).astype(bf16)


def weights_step(proj_block, update, weights):
    rows, cols = weights.shape
    ranks = proj_block.shape[1]
    width = cols // 4
    return pl.pallas_call(
        weights_kernel,
        grid=(4,),
        in_specs=[
            pl.BlockSpec((rows, ranks), lambda g: (0, 0)),
            pl.BlockSpec((ranks, width), lambda g: (0, g)),
            pl.BlockSpec((rows, width), lambda g: (0, g)),
        ],
        out_specs=pl.BlockSpec((rows, width), lambda g: (0, g)),
        out_shape=jax.ShapeDtypeStruct((rows, cols), bf16),
        compiler_params=pltpu.CompilerParams(vmem_limit_bytes=56 * MIB),
        cost_estimate=pl.CostEstimate(
            flops=2 * rows * cols * ranks, bytes_accessed=8000000, transcendentals=0
        ),
        name="weights",
    )(proj_block, update, weights)


def adam_rows(gradient, first, second):
    new_first = beta_first * first + (1.0 - beta_first) * gradient
    new_second = beta_second * second + (1.0 - beta_second) * gradient * gradient
    update = new_first * bias_first / (jnp.sqrt(new_second * bias_second) + epsilon)
    return (new_first, new_second, update.astype(bf16))


def body(layer_inputs, out_grads, projector, weights, moment_first, moment_second):
    blocks, block_width, tokens = layer_inputs.shape
    ranks = projector.shape[1]
    dp = lax.axis_index("dp")
    tensor = lax.axis_index("tensor")
    y, z, c = dp // (NZ * NC), (dp // NC) % NZ, dp % NC
    pos = jnp.stack([y, z, c]).astype(jnp.int32)

    rank = jnp.arange(ranks, dtype=jnp.int32)
    rank_p = (
        ((rank // 32 + y) % NY) * 64
        + ((rank // 8 + z) % NZ) * 16
        + ((rank // 128 + c) % NC) * 8
        + rank % 8
    )
    p_from_r = one_hot(rank_p, rank)

    proj_half = projector.astype(bf16)
    quarter = gather_ring(proj_half, send_z)
    x_rel = turn_blocks(pos, layer_inputs.reshape(NY, NZ, NC, block_width, tokens))
    quarter, x_rel = lax.optimization_barrier((quarter, x_rel))
    proj_rel = gather_ring(quarter, send_y)
    proj_rel = jnp.concatenate([proj_rel, send_core(proj_rel)], axis=0)

    latent_own = split_sum(lax.dot_general(proj_rel, x_rel, TN, preferred_element_type=f32))
    gram_part = lax.dot_general(proj_rel, proj_rel, TN, preferred_element_type=f32)
    latent = spread(latent_own)
    latent_p = jnp.dot(p_from_r, latent, preferred_element_type=f32).astype(bf16)

    grad_keep, grad_send = gradient_parts(latent_p, out_grads)
    total = grad_keep + send_core(grad_send).astype(f32)
    side = after((gram_part, proj_half), total)
    total = reduce_ring(total, send_y)
    for mask in (1, 2):
        side = side_step(*side, mask)
    total, *side = lax.optimization_barrier((total, *side))
    gradient, first_got = reduce_blocks(total, send_z)
    grad_half = gradient.astype(bf16)
    new_first, new_second, update = adam_rows(gradient, moment_first, moment_second)
    grad_own = gather_ring(grad_half, send_z)
    side = side_step(*side, 6)
    grad_own, gram_q, proj_rows = lax.optimization_barrier((grad_own, *side))
    update_all = lax.all_gather(update, "dp", axis=0, tiled=True)
    grad_own = gather_ring(grad_own, send_y)
    grad_p = jnp.concatenate([grad_own, send_core(grad_own)], axis=0)
    place = jnp.arange(8 * projector.shape[0], dtype=jnp.int32)
    block = place // block_width
    place_q = (block ^ ((block & 4) >> 1) ^ tensor) * block_width + place % block_width
    proj_block = jnp.dot(
        one_hot(place, place_q), proj_rows, preferred_element_type=f32
    ).astype(bf16)
    proj_block_p = lax.dot_general(
        proj_block, p_from_r, NT, preferred_element_type=f32
    ).astype(bf16)

    token_own = split_sum(lax.dot_general(grad_p, out_grads, NT, preferred_element_type=f32))
    gram_k = lax.dot_general(grad_p, grad_p, NT, preferred_element_type=f32).astype(bf16)
    second_part = jnp.dot(proj_block_p, gram_k, preferred_element_type=f32).astype(bf16)
    token_p, second = spread(token_own, second_part.reshape(NX * NL, -1, tokens))
    mix = 4.0 * jnp.eye(ranks, dtype=f32) - 2.0 * gram_q
    mix_p = jnp.concatenate(
        [
            jnp.dot(p_from_r, part, preferred_element_type=f32).astype(bf16)
            for part in split_high(mix)
        ],
        axis=0,
    )
    token_r = lax.dot_general(
        mix_p, jnp.concatenate([token_p, token_p], axis=0), TN, preferred_element_type=f32
    ).astype(bf16)

    n = x_rel.shape[0] // 2
    feat_send = lax.dot_general(x_rel[n:], token_r, NT, preferred_element_type=f32)
    feat_keep = lax.dot_general(x_rel[:n], token_r, NT, preferred_element_type=f32)
    total = feat_keep + send_core(feat_send.astype(bf16)).astype(f32)
    total = reduce_ring(total, send_y)
    new_weights = weights_step(proj_block, update_all, weights)
    feature_sum = reduce_blocks(total, send_z, new_weights)[0]

    second = jnp.sum(second.astype(f32), axis=0).reshape(block_width, ranks)
    second = jnp.dot(second, p_from_r.astype(f32), precision=HIGHEST)
    increment = proj_rate * (feature_sum - 2.0 * second)
    return (new_weights, new_first, new_second, increment)


def solution(mesh):
    placed = (
        P(None, "tensor", "dp"),
        P("dp", "tensor"),
        P(("dp", "tensor"), None),
        P("dp", "tensor"),
        P("dp", "tensor"),
        P("dp", "tensor"),
    )
    return jax.shard_map(
        body,
        mesh=mesh,
        in_specs=placed,
        out_specs=(
            P("dp", "tensor"),
            P("dp", "tensor"),
            P("dp", "tensor"),
            P(("dp", "tensor"), None),
        ),
        check_vma=False,
    )
```

```python
import jax
import jax.numpy as jnp
from jax import lax
from jax.experimental import pallas as pl
from jax.experimental.pallas import tpu as pltpu
from jax.sharding import PartitionSpec as P

beta_first = 0.9
beta_second = 0.999
bias_first = 1.0 / (1.0 - 0.9**10)
bias_second = 1.0 / (1.0 - 0.999**10)
epsilon = 1e-08
weight_rate = 2.0
proj_rate = 0.0002

bf16 = jnp.bfloat16
f32 = jnp.float32
HIGHEST = lax.Precision.HIGHEST
NY, NZ, NC = 4, 4, 2
NX, NL = 4, 2
TN = (((0,), (0,)), ((), ()))
NT = (((1,), (1,)), ((), ()))
MIB = 1024 * 1024


def dp_pairs(dy, dz, dc):
    return [
        (
            (y * NZ + z) * NC + c,
            (((y + dy) % NY) * NZ + (z + dz) % NZ) * NC + (c + dc) % NC,
        )
        for y in range(NY)
        for z in range(NZ)
        for c in range(NC)
    ]


def send_y(block, k):
    return lax.ppermute(block, "dp", dp_pairs(k, 0, 0))


def send_z(block, k):
    return lax.ppermute(block, "dp", dp_pairs(0, k, 0))


def send_core(block):
    return lax.ppermute(block, "dp", dp_pairs(0, 0, 1))


def send_xor(block, bit):
    return lax.ppermute(block, "tensor", [(j, j ^ bit) for j in range(NX * NL)])


def ring_blocks(block, send):
    got = {k: send(block, k) for k in (2, 1, 3)}
    return jnp.concatenate([block, got[3], got[2], got[1]], axis=0), got[1]


def gather_ring(block, send):
    return ring_blocks(block, send)[0]


def after(value, trigger):
    return lax.optimization_barrier((value, trigger))[0]


def split_high(value):
    high = value.astype(bf16)
    return high, (value - high.astype(f32)).astype(bf16)


def side_step(gram, rows, mask, trigger=None):
    n = gram.shape[0]
    eye = jnp.eye(n, dtype=f32)
    high, low = split_high(gram)
    rest = jnp.sum(low.astype(f32) * eye, axis=0).astype(bf16)
    payload = jnp.concatenate([high, jnp.broadcast_to(rest, (16, n)), rows], axis=0)
    if trigger is not None:
        payload = after(payload, trigger)
    got = send_xor(payload, mask)
    gram = gram + got[:n].astype(f32) + eye * got[n : n + 1].astype(f32)
    return gram, jnp.concatenate([rows, got[n + 16 :]], axis=0)


def split_sum(part, extra=None):
    n = NX * NL
    rows, cols = part.shape
    share = rows // n
    blocks = part.astype(bf16).reshape(n, share, cols)
    if extra is not None:
        high, wide = extra.shape
        extra = jnp.pad(extra.astype(bf16), ((0, 16 - high), (0, cols - wide)))
        blocks = jnp.concatenate([blocks, jnp.broadcast_to(extra, (n, 16, cols))], axis=1)
    got = lax.all_to_all(blocks, "tensor", 0, 0)
    own = jnp.sum(got[:, :share].astype(f32), axis=0).astype(bf16)
    if extra is None:
        return own
    return own, jnp.sum(got[:, share : share + high, :wide].astype(f32), axis=0)


def spread(own):
    n = NX * NL
    rows, cols = own.shape
    blocks = jnp.broadcast_to(own, (n, rows, cols))
    return lax.all_to_all(blocks, "tensor", 0, 0).reshape(n * rows, cols)


def reduce_blocks(rows, send, beside=None):
    n = rows.shape[0] // 4
    got = [send(rows[k * n : (k + 1) * n].astype(bf16), k) for k in (2, 1, 3)]
    total = rows[:n].astype(f32)
    if beside is not None:
        total = after(total, beside)
    for block in got:
        total = total + block.astype(f32)
    return total, got[1]


def reduce_ring(rows, send):
    return reduce_blocks(rows, send)[0]


def one_hot(left, right):
    return (left[:, None] == right[None, :]).astype(bf16)


def turn_kernel(pos, x_ref, out_ref):
    z = pos[1]
    n = x_ref.shape[3]
    for k in range(NZ):
        out_ref[pl.ds(k * n, n), :] = x_ref[0, lax.rem(z + k, NZ), 0]


def turn_blocks(pos, x_view):
    block_width, tokens = x_view.shape[3:]
    rows = NZ * block_width
    return pl.pallas_call(
        turn_kernel,
        grid_spec=pltpu.PrefetchScalarGridSpec(
            num_scalar_prefetch=1,
            grid=(NC * NY,),
            in_specs=[
                pl.BlockSpec(
                    (1, NZ, 1, block_width, tokens),
                    lambda g, pos: (
                        lax.rem(pos[0] + lax.rem(g, NY), NY),
                        0,
                        lax.rem(pos[2] + lax.div(g, NY), NC),
                        0,
                        0,
                    ),
                ),
            ],
            out_specs=pl.BlockSpec((rows, tokens), lambda g, pos: (g, 0)),
        ),
        out_shape=jax.ShapeDtypeStruct((NC * NY * rows, tokens), bf16),
        compiler_params=pltpu.CompilerParams(vmem_limit_bytes=24 * MIB),
        cost_estimate=pl.CostEstimate(flops=0, bytes_accessed=12000000, transcendentals=0),
        name="turn",
    )(pos, x_view)


def gradient_kernel(latent_ref, cot_ref, keep_ref, send_ref):
    half = keep_ref.shape[0]
    for at in range(0, cot_ref.shape[1], 512):
        cols = pl.ds(at, 512)
        part = jnp.dot(latent_ref[...], cot_ref[:, cols], preferred_element_type=f32)
        keep_ref[:, cols] = part[:half]
        send_ref[:, cols] = part[half:].astype(bf16)


def gradient_parts(latent, out_grads):
    ranks, tokens = latent.shape
    cols = out_grads.shape[1]
    half = ranks // 2
    local = pl.BlockSpec(memory_space=pltpu.VMEM)
    return pl.pallas_call(
        gradient_kernel,
        in_specs=[local, local],
        out_specs=[local, local],
        out_shape=[
            jax.ShapeDtypeStruct((half, cols), f32),
            jax.ShapeDtypeStruct((half, cols), bf16),
        ],
        compiler_params=pltpu.CompilerParams(vmem_limit_bytes=24 * MIB),
        cost_estimate=pl.CostEstimate(
            flops=2 * ranks * tokens * cols, bytes_accessed=6500000, transcendentals=0
        ),
        name="gradient",
    )(latent, out_grads)


def weights_kernel(proj_ref, update_ref, weights_ref, out_ref):
    change = jnp.dot(proj_ref[...], update_ref[...], preferred_element_type=f32)
    out_ref[...] = (weights_ref[...].astype(f32) - weight_rate * change).astype(bf16)


def weights_step(proj_block, update, weights):
    rows, cols = weights.shape
    ranks = proj_block.shape[1]
    width = cols // 4
    return pl.pallas_call(
        weights_kernel,
        grid=(4,),
        in_specs=[
            pl.BlockSpec((rows, ranks), lambda g: (0, 0)),
            pl.BlockSpec((ranks, width), lambda g: (0, g)),
            pl.BlockSpec((rows, width), lambda g: (0, g)),
        ],
        out_specs=pl.BlockSpec((rows, width), lambda g: (0, g)),
        out_shape=jax.ShapeDtypeStruct((rows, cols), bf16),
        compiler_params=pltpu.CompilerParams(vmem_limit_bytes=56 * MIB),
        cost_estimate=pl.CostEstimate(
            flops=2 * rows * cols * ranks, bytes_accessed=8000000, transcendentals=0
        ),
        name="weights",
    )(proj_block, update, weights)


def adam_rows(gradient, first, second):
    new_first = beta_first * first + (1.0 - beta_first) * gradient
    new_second = beta_second * second + (1.0 - beta_second) * gradient * gradient
    update = new_first * bias_first / (jnp.sqrt(new_second * bias_second) + epsilon)
    return (new_first, new_second, update.astype(bf16))


def body(layer_inputs, out_grads, projector, weights, moment_first, moment_second):
    blocks, block_width, tokens = layer_inputs.shape
    ranks = projector.shape[1]
    dp = lax.axis_index("dp")
    tensor = lax.axis_index("tensor")
    y, z, c = dp // (NZ * NC), (dp // NC) % NZ, dp % NC
    pos = jnp.stack([y, z, c]).astype(jnp.int32)

    rank = jnp.arange(ranks, dtype=jnp.int32)
    rank_p = (
        ((rank // 32 + y) % NY) * 64
        + ((rank // 8 + z) % NZ) * 16
        + ((rank // 128 + c) % NC) * 8
        + rank % 8
    )
    p_from_r = one_hot(rank_p, rank)

    proj_half = projector.astype(bf16)
    quarter = gather_ring(proj_half, send_z)
    x_rel = turn_blocks(pos, layer_inputs.reshape(NY, NZ, NC, block_width, tokens))
    quarter, x_rel = lax.optimization_barrier((quarter, x_rel))
    proj_rel = gather_ring(quarter, send_y)
    proj_rel = jnp.concatenate([proj_rel, send_core(proj_rel)], axis=0)

    latent_own = split_sum(lax.dot_general(proj_rel, x_rel, TN, preferred_element_type=f32))
    gram_part = lax.dot_general(proj_rel, proj_rel, TN, preferred_element_type=f32)
    latent = spread(latent_own)
    latent_p = jnp.dot(p_from_r, latent, preferred_element_type=f32).astype(bf16)

    grad_keep, grad_send = gradient_parts(latent_p, out_grads)
    total = grad_keep + send_core(grad_send).astype(f32)
    side = side_step(*side_step(gram_part, proj_half, 1, total), 2)
    total, *side = lax.optimization_barrier((reduce_ring(total, send_y), *side))
    gradient = reduce_ring(total, send_z)
    grad_half = gradient.astype(bf16)
    new_first, new_second, update = adam_rows(gradient, moment_first, moment_second)
    grad_own = gather_ring(grad_half, send_z)
    side = side_step(*side, 6)
    grad_own, gram_q, proj_rows = lax.optimization_barrier((grad_own, *side))
    update_all = lax.all_gather(update, "dp", axis=0, tiled=True)
    grad_own = gather_ring(grad_own, send_y)
    grad_p = jnp.concatenate([grad_own, send_core(grad_own)], axis=0)
    place = jnp.arange(8 * projector.shape[0], dtype=jnp.int32)
    block = place // block_width
    place_q = (block ^ ((block & 4) >> 1) ^ tensor) * block_width + place % block_width
    proj_block = jnp.dot(
        one_hot(place, place_q), proj_rows, preferred_element_type=f32
    ).astype(bf16)

    token_part = lax.dot_general(grad_p, out_grads, NT, preferred_element_type=f32)
    gram_rows = lax.dot_general(grad_half, grad_p, NT, preferred_element_type=f32)
    mix = 4.0 * jnp.eye(ranks, dtype=f32) - 2.0 * gram_q
    mix_p = jnp.concatenate(
        [
            jnp.dot(p_from_r, part, preferred_element_type=f32).astype(bf16)
            for part in split_high(mix)
        ],
        axis=0,
    )
    token_own, gram_rows = split_sum(token_part, gram_rows)
    token_own, proj_block = lax.optimization_barrier((token_own, proj_block))
    token_p = spread(token_own)
    own_rank = lax.axis_index("dp") * 8 + jnp.arange(8, dtype=jnp.int32)
    gram_rows = jnp.dot((-2.0 * gram_rows).astype(bf16), p_from_r, preferred_element_type=f32)
    gram_place = jnp.dot(
        one_hot(rank, own_rank), gram_rows.astype(bf16), preferred_element_type=f32
    ).astype(bf16)
    token_r = lax.dot_general(
        mix_p, jnp.concatenate([token_p, token_p], axis=0), TN, preferred_element_type=f32
    ).astype(bf16)

    n = x_rel.shape[0] // 2
    feat_send, feat_keep = [
        lax.dot_general(x_rel[part], token_r, NT, preferred_element_type=f32)
        + jnp.dot(proj_rel[part], gram_place, preferred_element_type=f32)
        for part in (slice(n, None), slice(0, n))
    ]
    total = feat_keep + send_core(feat_send.astype(bf16)).astype(f32)
    total = reduce_ring(total, send_y)
    new_weights = weights_step(proj_block, update_all, weights)
    feature_sum = reduce_blocks(total, send_z, new_weights)[0]

    increment = proj_rate * feature_sum
    return (new_weights, new_first, new_second, increment)


def solution(mesh):
    placed = (
        P(None, "tensor", "dp"),
        P("dp", "tensor"),
        P(("dp", "tensor"), None),
        P("dp", "tensor"),
        P("dp", "tensor"),
        P("dp", "tensor"),
    )
    return jax.shard_map(
        body,
        mesh=mesh,
        in_specs=placed,
        out_specs=(
            P("dp", "tensor"),
            P("dp", "tensor"),
            P("dp", "tensor"),
            P(("dp", "tensor"), None),
        ),
        check_vma=False,
    )
```
